32 devices in a mesh: diag: 16 (over z, y, core), tri: 2 (over x).
Axes of the slice: x: 2, y: 2, z: 4, core: 2. Of those that a mesh axis runs over, the one named last changes fastest.
Arguments:
- trial_sets: bfloat16 [2, 12, 65536], P(None, None, 'diag'), may hold values from -6 to 6
- tile_values: bfloat16 [16, 2, 192, 128, 128], P('diag', 'tri'), may hold values from -0.109375 to 0.109375
- tile_pattern: int32 [16, 2, 2, 192], P('diag', 'tri'), may hold values from 0 to 31, as said below
- tile_count: int32 [16, 2], P('diag', 'tri'), may hold values from 48 to 192, as said below
Outputs:
- images: float32 [2, 12, 65536], P(None, None, ('diag', 'tri'))
The draws below stay inside these ranges and needn't reach their ends.
Inputs may be any that keep to these rules, and one draw needn't show every extreme that they name: `tile_pattern`: within each stored block the live and padding slots name distinct tiles. `tile_count`: some stored block has all 192 slots live.
All inputs are finite; a program needn't handle non-finite values.
Results may differ from the reference program's by a relative error of at most 0.0003.
Values may be sent and summed in bfloat16 or wider, within the bound.
No kernel may reach another device: no remote copies, remote signals or barrier semaphores. Data moves between devices by JAX's collectives and lax.ppermute only.
A program may use at most 64 MiB of HBM per device.

```python
import jax
import jax.numpy as jnp
from jax import lax

TILE = 128
SETS = 2
VECS = 12
BLOCK_TILES = 32
OWNER_TILES = 192
ROWS = 65536
N_DIAG = 16
N_TRI = 2


def draw_tile_pattern(key, part):
    owner_keys = jax.random.split(key, N_DIAG * N_TRI)
    chosen = jax.vmap(lambda subkey: jax.random.permutation(subkey, BLOCK_TILES * BLOCK_TILES)[:OWNER_TILES])(owner_keys)
    chosen = chosen.reshape(N_DIAG, N_TRI, OWNER_TILES).astype(jnp.int32)
    return jnp.stack([chosen // BLOCK_TILES, chosen % BLOCK_TILES], axis=2).astype(jnp.int32)


def draw_tile_count(key, part):
    first_key, second_key = jax.random.split(key)
    counts = jax.random.randint(first_key, (N_DIAG * N_TRI,), OWNER_TILES // 4, OWNER_TILES + 1)
    fullest = jax.random.randint(second_key, (), 0, N_DIAG * N_TRI)
    counts = jnp.where(jnp.arange(N_DIAG * N_TRI) == fullest, OWNER_TILES, counts)
    return counts.reshape(N_DIAG, N_TRI).astype(jnp.int32)


def shard_levels(stream_key, extent, cuts, smallest, largest):
    factor_of, own = 1.0, jax.random.fold_in(stream_key, 6)
    for dim, parts in cuts:
        heights = jnp.exp(jax.random.uniform(jax.random.fold_in(own, dim), (parts,), jnp.float32, smallest / len(cuts), largest / len(cuts)))
        factor_of = factor_of * jnp.repeat(heights, extent[dim] // parts).reshape([-1 if axis == dim else 1 for axis in range(len(extent))])
    return factor_of


def centred(key, extent, scale, most, cuts=(), dtype=jnp.bfloat16):
    array = scale * jax.random.normal(key, extent, jnp.float32)
    if cuts:
        array = array * shard_levels(key, extent, cuts, -0.22, 0.18)
    return jnp.clip(array, -most, most).astype(dtype)


def setup_inputs(seed: int = 0) -> dict:
    seeds = jax.random.split(jax.random.key(seed), 5)
    trial_sets = centred(seeds[0], (SETS, VECS, ROWS), 1.0, 6.0, ((2, 16),))
    tile_values = centred(seeds[1], (N_DIAG, N_TRI, OWNER_TILES, TILE, TILE), (2 * N_TRI * OWNER_TILES * TILE // BLOCK_TILES) ** -0.5, 0.109375, ((0, 16), (1, 2)))
    tile_pattern = draw_tile_pattern(jax.random.fold_in(seeds[4], 71), 0)
    tile_count = draw_tile_count(jax.random.fold_in(seeds[4], 71), 0)
    return {"trial_sets": trial_sets, "tile_values": tile_values, "tile_pattern": tile_pattern, "tile_count": tile_count}


def reference(trial_sets, tile_values, tile_pattern, tile_count):
    set_count, vec_count, row_total = trial_sets.shape
    columns = set_count * vec_count
    grid = trial_sets.astype(jnp.float32).reshape(columns, N_DIAG, BLOCK_TILES, TILE)
    tile_axis = jnp.arange(BLOCK_TILES)
    slot_axis = jnp.arange(OWNER_TILES)

    def per_diag(diag_index):
        row_sum = jnp.zeros((columns, BLOCK_TILES, TILE), jnp.float32)
        col_list = []
        own_block = grid[:, diag_index]
        for tri_index in range(N_TRI):
            tile_data = tile_values[diag_index, tri_index].astype(jnp.float32)
            tile_rows = tile_pattern[diag_index, tri_index, 0]
            tile_cols = tile_pattern[diag_index, tri_index, 1]
            live_mask = (slot_axis < tile_count[diag_index, tri_index]).astype(jnp.float32)
            source = (diag_index - tri_index) % N_DIAG
            held_block = grid[:, source]
            picked_cols = held_block[:, tile_cols, :]
            row_terms = jnp.einsum("nab,vnb->vna", tile_data, picked_cols, precision=lax.Precision.HIGHEST)
            row_hot = (tile_rows[:, None] == tile_axis[None, :]).astype(jnp.float32) * live_mask[:, None]
            row_sum = row_sum + jnp.einsum("vna,nr->vra", row_terms, row_hot, precision=lax.Precision.HIGHEST)
            picked_rows = own_block[:, tile_rows, :]
            col_terms = jnp.einsum("nab,vna->vnb", tile_data, picked_rows, precision=lax.Precision.HIGHEST)
            col_hot = (tile_cols[:, None] == tile_axis[None, :]).astype(jnp.float32) * live_mask[:, None]
            col_list.append(jnp.einsum("vnb,nr->vrb", col_terms, col_hot, precision=lax.Precision.HIGHEST))
        return row_sum, jnp.stack(col_list)

    row_all, col_all = lax.map(per_diag, jnp.arange(N_DIAG))
    combined = row_all
    for tri_index in range(N_TRI):
        combined = combined + jnp.roll(col_all[:, tri_index], -tri_index, axis=0)
    return combined.transpose(1, 0, 2, 3).reshape(set_count, vec_count, row_total)
```

```python
import functools
import math

import jax
import jax.numpy as jnp
from jax import lax
from jax.experimental import pallas as pl
from jax.experimental.pallas import tpu as pltpu
from jax.sharding import PartitionSpec as P

F32 = jnp.float32
VMEM_BYTES = 56 << 20


def fill_vectors(vectors_ref, packed_ref, tile):
    blocks, padded, _ = packed_ref.shape
    vecs, sets, _ = vectors_ref.shape
    for b in range(blocks):
        slab = vectors_ref[:, :, b * tile : (b + 1) * tile].reshape(vecs * sets, tile)
        packed_ref[b] = jnp.concatenate(
            [slab, jnp.zeros((padded - vecs * sets, tile), slab.dtype)], axis=0
        )


def add_products(group, count, pattern_ref, packed_ref, tiles_ref, sums_ref, by_row, by_col):
    blocks, columns, tile = sums_ref.shape
    blocks -= 1
    padded = packed_ref.shape[1]
    size = group[1]
    results = []
    for u in range(0, size, 2):
        s = group[0] * size + u
        rows = [pattern_ref[0, s + e] for e in range(2)]
        cols = [pattern_ref[1, s + e] for e in range(2)]
        live = [s + e < count for e in range(2)]
        pair = tiles_ref[pl.ds(s, 2)]
        if by_col:
            left = jnp.concatenate([packed_ref[rows[0]], packed_ref[rows[1]]], axis=0)
            right = jnp.concatenate([pair[0], pair[1]], axis=1)
            both = jnp.dot(left, right, preferred_element_type=F32)
            for e in range(2):
                part = both[e * padded : e * padded + columns, e * tile : (e + 1) * tile]
                results.append((jnp.where(live[e], cols[e], blocks), part))
        if by_row:
            left = jnp.concatenate([packed_ref[cols[0]], packed_ref[cols[1]]], axis=0)
            right = pair.reshape(2 * tile, tile)
            both = lax.dot_general(
                left, right, (((1,), (1,)), ((), ())), preferred_element_type=F32
            )
            for e in range(2):
                part = both[e * padded : e * padded + columns, e * tile : (e + 1) * tile]
                results.append((jnp.where(live[e], rows[e], blocks), part))
    for place, part in results:
        sums_ref[place] += part


def first_kernel(
    chunk, count_hbm, pattern_hbm, vectors_hbm, tiles_hbm,
    own_ref, tiles_ref, *rest,
):
    messages, (count_ref, pattern_ref, vectors_ref, packed_ref, sums_ref, small_sem, tile_sem) = rest[:-7], rest[-7:]
    tile_total = tiles_ref.shape[0]
    chunks = tile_total // chunk
    tri_index = lax.axis_index("tri")
    loads = [
        pltpu.make_async_copy(vectors_hbm, vectors_ref, small_sem.at[0]),
        pltpu.make_async_copy(pattern_hbm.at[0, 0], pattern_ref, small_sem.at[1]),
        pltpu.make_async_copy(count_hbm, count_ref, small_sem.at[2]),
    ]
    streams = [
        pltpu.make_async_copy(
            tiles_hbm.at[0, 0, pl.ds(k * chunk, chunk)], tiles_ref.at[pl.ds(k * chunk, chunk)], tile_sem.at[k]
        )
        for k in range(chunks)
    ]
    for copy in loads + streams:
        copy.start()
    sums_ref[...] = jnp.zeros_like(sums_ref)
    for copy in loads:
        copy.wait()
    fill_vectors(vectors_ref, packed_ref, tiles_ref.shape[1])
    count = count_ref[0, 0]
    refs = (pattern_ref, packed_ref, tiles_ref, sums_ref)
    for k in range(chunks):
        streams[k].wait()

        @pl.when((count > k * chunk) & (tri_index == 0))
        def _():
            add_products((k, chunk), count, *refs, True, True)

        @pl.when((count > k * chunk) & (tri_index != 0))
        def _():
            add_products((k, chunk), count, *refs, False, True)

    blocks = packed_ref.shape[0]
    parts = len(messages)
    held = blocks // parts

    @pl.when(tri_index == 0)
    def _():
        own_ref[...] = sums_ref[:blocks]

    @pl.when(tri_index != 0)
    def _():
        for d, message_ref in enumerate(messages):
            part = lax.rem(tri_index + d, parts)
            message_ref[...] = sums_ref[pl.ds(part * held, held)]


def second_kernel(chunk, count_hbm, pattern_hbm, vectors_hbm, tiles_ref, own_ref, keep_ref, *rest):
    messages, (count_ref, pattern_ref, vectors_ref, packed_ref, sums_ref, small_sem) = rest[:-6], rest[-6:]
    chunks = tiles_ref.shape[0] // chunk
    tri_index = lax.axis_index("tri")
    blocks = packed_ref.shape[0]
    parts = len(messages) + 1
    held = blocks // parts
    loads = [
        pltpu.make_async_copy(vectors_hbm, vectors_ref, small_sem.at[0]),
        pltpu.make_async_copy(pattern_hbm.at[0, 0], pattern_ref, small_sem.at[1]),
        pltpu.make_async_copy(count_hbm, count_ref, small_sem.at[2]),
    ]
    for copy in loads:
        copy.start()
    sums_ref[...] = jnp.zeros_like(sums_ref)
    for copy in loads:
        copy.wait()

    def hand_out(source):
        keep_ref[...] = source[pl.ds(tri_index * held, held)]
        for d, message_ref in enumerate(messages):
            part = lax.rem(tri_index + d + 1, parts)
            message_ref[...] = source[pl.ds(part * held, held)]

    @pl.when(tri_index == 0)
    def _():
        hand_out(own_ref)

    @pl.when(tri_index != 0)
    def _():
        fill_vectors(vectors_ref, packed_ref, tiles_ref.shape[1])
        count = count_ref[0, 0]
        for k in range(chunks):

            @pl.when(count > k * chunk)
            def _():
                add_products((k, chunk), count, pattern_ref, packed_ref, tiles_ref, sums_ref, True, False)

        hand_out(sums_ref)


def last_kernel(parts, keep_ref, *rest):
    *messages, out_ref, total_ref = rest
    tri_index = lax.axis_index("tri")
    blocks, _, tile = keep_ref.shape
    total_ref[...] = keep_ref[...]
    for message_ref in messages[: parts - 1]:
        total_ref[...] += message_ref[...]
    for d, message_ref in enumerate(messages[parts - 1 :]):

        @pl.when(lax.rem(tri_index + parts - d, parts) != 0)
        def _(message_ref=message_ref):
            total_ref[...] += message_ref[...]

    vecs, sets, _ = out_ref.shape
    for b in range(blocks):
        out_ref[:, :, b * tile : (b + 1) * tile] = total_ref[b].reshape(vecs, sets, tile)


def local(trial_sets, tile_values, tile_pattern, tile_count):
    set_count, vec_count, row_total = trial_sets.shape
    columns = set_count * vec_count
    tile_total, tile = tile_values.shape[2:4]
    blocks = row_total // tile
    chunk = math.gcd(tile_total, 32)
    chunks = tile_total // chunk
    parts = lax.axis_size("tri")
    ring = lax.axis_size("diag")
    held = blocks // parts
    padded = -(-columns // 16) * 16
    message = jax.ShapeDtypeStruct((held, columns, tile), F32)
    smem, vmem, hbm = (pl.BlockSpec(memory_space=m) for m in (pltpu.SMEM, pltpu.VMEM, pltpu.HBM))
    small = [
        pltpu.SMEM((1, 1), jnp.int32),
        pltpu.SMEM((2, tile_total), jnp.int32),
        pltpu.VMEM((vec_count, set_count, row_total), jnp.bfloat16),
        pltpu.VMEM((blocks, padded, tile), jnp.bfloat16),
        pltpu.VMEM((blocks + 1, columns, tile), F32),
        pltpu.SemaphoreType.DMA((3,)),
    ]
    params = pltpu.CompilerParams(vmem_limit_bytes=VMEM_BYTES)

    def moved(x, shift, turn):
        pairs = [
            (i * parts + t, (i + shift(t)) % ring * parts + (t + turn) % parts)
            for i in range(ring)
            for t in range(parts)
        ]
        return lax.ppermute(x, ("diag", "tri"), pairs)

    vectors = trial_sets.transpose(1, 0, 2)
    offset = lambda t: max(t, 1)
    passed = moved(vectors, offset, 0)
    own, tiles, *back = pl.pallas_call(
        functools.partial(first_kernel, chunk),
        out_shape=[
            jax.ShapeDtypeStruct((blocks, columns, tile), F32),
            jax.ShapeDtypeStruct((tile_total, tile, tile), tile_values.dtype),
        ]
        + [message] * parts,
        in_specs=[hbm] * 4,
        out_specs=[vmem] * (2 + parts),
        scratch_shapes=small + [pltpu.SemaphoreType.DMA((chunks,))],
        compiler_params=params,
        name="transposed_products",
    )(tile_count, tile_pattern, vectors, tile_values)
    back = [moved(m, lambda t: -offset(t), d) for d, m in enumerate(back)]
    keep, *across = pl.pallas_call(
        functools.partial(second_kernel, chunk),
        out_shape=[jax.ShapeDtypeStruct((held, columns, tile), F32)] + [message] * (parts - 1),
        in_specs=[hbm] * 3 + [vmem] * 2,
        out_specs=[vmem] * parts,
        scratch_shapes=small,
        compiler_params=params,
        name="plain_products",
    )(tile_count, tile_pattern, passed, tiles, own)
    across = [moved(m, lambda t: 0, d + 1) for d, m in enumerate(across)]
    images = pl.pallas_call(
        functools.partial(last_kernel, parts),
        out_shape=jax.ShapeDtypeStruct((vec_count, set_count, row_total // parts), F32),
        in_specs=[vmem] * (2 * parts),
        out_specs=vmem,
        scratch_shapes=[pltpu.VMEM((held, columns, tile), F32)],
        compiler_params=params,
        name="sum_of_parts",
    )(keep, *across, *back)
    return images.transpose(1, 0, 2)


def solution(mesh):
    return jax.shard_map(
        local,
        mesh=mesh,
        in_specs=(
            P(None, None, "diag"),
            P("diag", "tri", None, None, None),
            P("diag", "tri", None, None),
            P("diag", "tri"),
        ),
        out_specs=P(None, None, ("diag", "tri")),
        check_vma=False,
    )
```

```python
import functools
import math

import jax
import jax.numpy as jnp
from jax import lax
from jax.experimental import pallas as pl
from jax.experimental.pallas import tpu as pltpu
from jax.sharding import PartitionSpec as P

F32 = jnp.float32
VMEM_BYTES = 16 << 20
WIDE_BYTES = 24 << 20
AHEAD = 3


def fill_vectors(vectors_ref, packed_ref, tile):
    blocks, padded, _ = packed_ref.shape
    vecs, sets, _ = vectors_ref.shape
    for b in range(blocks):
        slab = vectors_ref[:, :, b * tile : (b + 1) * tile].reshape(vecs * sets, tile)
        packed_ref[b] = jnp.concatenate(
            [slab, jnp.zeros((padded - vecs * sets, tile), slab.dtype)], axis=0
        )


def add_products(start, size, count, pattern_ref, packed_ref, tiles_ref, sums_ref, by_row, by_col):
    blocks, columns, tile = sums_ref.shape
    blocks -= 1
    padded = packed_ref.shape[1]
    results = []
    for u in range(0, size, 2):
        s = start + u
        rows = [pattern_ref[0, s + e] for e in range(2)]
        cols = [pattern_ref[1, s + e] for e in range(2)]
        live = [s + e < count for e in range(2)]
        pair = tiles_ref[pl.ds(s, 2)]
        if by_col:
            left = jnp.concatenate([packed_ref[rows[0]], packed_ref[rows[1]]], axis=0)
            right = jnp.concatenate([pair[0], pair[1]], axis=1)
            both = jnp.dot(left, right, preferred_element_type=F32)
            for e in range(2):
                part = both[e * padded : e * padded + columns, e * tile : (e + 1) * tile]
                results.append((jnp.where(live[e], cols[e], blocks), part))
        if by_row:
            left = jnp.concatenate([packed_ref[cols[0]], packed_ref[cols[1]]], axis=0)
            right = pair.reshape(2 * tile, tile)
            both = lax.dot_general(
                left, right, (((1,), (1,)), ((), ())), preferred_element_type=F32
            )
            for e in range(2):
                part = both[e * padded : e * padded + columns, e * tile : (e + 1) * tile]
                results.append((jnp.where(live[e], rows[e], blocks), part))
    for place, part in results:
        sums_ref[place] += part


def first_kernel(steps, count_ref, pattern_hbm, vectors_hbm, tiles_hbm, *rest):
    tiles_ref, *messages = rest[:-6]
    pattern_ref, vectors_ref, packed_ref, sums_ref, small_sem, tile_sem = rest[-6:]
    parts = len(messages)
    blocks = packed_ref.shape[0]
    held = blocks // parts
    tri_index = lax.axis_index("tri")
    loads = [
        pltpu.make_async_copy(vectors_hbm, vectors_ref, small_sem.at[0]),
        pltpu.make_async_copy(pattern_hbm.at[0, 0], pattern_ref, small_sem.at[1]),
    ]
    streams = [
        pltpu.make_async_copy(
            tiles_hbm.at[0, 0, pl.ds(start, size)], tiles_ref.at[pl.ds(start, size)], tile_sem.at[k]
        )
        for k, (start, size) in enumerate(steps)
    ]
    for copy in loads + streams[:AHEAD]:
        copy.start()
    sums_ref[...] = jnp.zeros_like(sums_ref)
    for copy in loads:
        copy.wait()
    fill_vectors(vectors_ref, packed_ref, tiles_ref.shape[1])
    count = count_ref[0, 0]
    for k, (start, size) in enumerate(steps):
        streams[k].wait()
        if k + AHEAD < len(steps):
            streams[k + AHEAD].start()

        @pl.when(count > start)
        def _():
            add_products(start, size, count, pattern_ref, packed_ref, tiles_ref, sums_ref, False, True)

    for d, message_ref in enumerate(messages):
        part = lax.rem(tri_index + d, parts)
        message_ref[...] = sums_ref[pl.ds(part * held, held)]


def second_kernel(steps, count_ref, pattern_ref, vectors_ref, passed_ref, tiles_ref, *rest):
    half = (len(rest) - 2) // 2
    own, messages, (packed_ref, sums_ref) = rest[:half], rest[half:-2], rest[-2:]
    parts = len(messages)
    blocks = packed_ref.shape[0]
    held = blocks // parts
    tri_index = lax.axis_index("tri")

    @pl.when(tri_index == 0)
    def _():
        for d, own_ref in enumerate(own):
            sums_ref[d * held : (d + 1) * held] = own_ref[...]
        fill_vectors(vectors_ref, packed_ref, tiles_ref.shape[1])

    @pl.when(tri_index != 0)
    def _():
        sums_ref[...] = jnp.zeros_like(sums_ref)
        fill_vectors(passed_ref, packed_ref, tiles_ref.shape[1])

    count = count_ref[0, 0]
    for start, size in steps:

        @pl.when(count > start)
        def _():
            add_products(start, size, count, pattern_ref, packed_ref, tiles_ref, sums_ref, True, False)

    for d, message_ref in enumerate(messages):
        part = lax.rem(tri_index + d, parts)
        message_ref[...] = sums_ref[pl.ds(part * held, held)]


def last_kernel(parts, keep_ref, *rest):
    *messages, out_ref, total_ref = rest
    tri_index = lax.axis_index("tri")
    blocks, _, tile = keep_ref.shape
    total_ref[...] = keep_ref[...]
    for message_ref in messages[: parts - 1]:
        total_ref[...] += message_ref[...]
    for d, message_ref in enumerate(messages[parts - 1 :]):

        @pl.when(lax.rem(tri_index + parts - d, parts) != 0)
        def _(message_ref=message_ref):
            total_ref[...] += message_ref[...]

    vecs, sets, _ = out_ref.shape
    for b in range(blocks):
        out_ref[:, :, b * tile : (b + 1) * tile] = total_ref[b].reshape(vecs, sets, tile)


def local(trial_sets, tile_values, tile_pattern, tile_count):
    set_count, vec_count, row_total = trial_sets.shape
    columns = set_count * vec_count
    tile_total, tile = tile_values.shape[2:4]
    blocks = row_total // tile
    unit = math.gcd(tile_total, 32)
    steps = [(k * unit, unit) for k in range(tile_total // unit)]
    half = tile_total // 2
    halves = [(0, half), (half, half)]
    parts = lax.axis_size("tri")
    ring = lax.axis_size("diag")
    held = blocks // parts
    padded = -(-columns // 16) * 16
    message = pltpu.VMEM((held, columns, tile), F32)
    smem, vmem, hbm = (pl.BlockSpec(memory_space=m) for m in (pltpu.SMEM, pltpu.VMEM, pltpu.HBM))
    scratch = [
        pltpu.VMEM((blocks, padded, tile), jnp.bfloat16),
        pltpu.VMEM((blocks + 1, columns, tile), F32),
    ]
    params = pltpu.CompilerParams(vmem_limit_bytes=VMEM_BYTES)

    def moved(x, shift, turn):
        pairs = [
            (i * parts + t, (i + shift(t)) % ring * parts + (t + turn) % parts)
            for i in range(ring)
            for t in range(parts)
        ]
        return lax.ppermute(x, ("diag", "tri"), pairs)

    vectors = trial_sets.transpose(1, 0, 2)
    offset = lambda t: max(t, 1)
    passed = moved(vectors, offset, 0)
    pattern = tile_pattern.reshape(2, tile_total)
    tiles, *own = pl.pallas_call(
        functools.partial(first_kernel, steps),
        out_shape=[pltpu.VMEM((tile_total, tile, tile), tile_values.dtype)] + [message] * parts,
        in_specs=[smem] + [hbm] * 3,
        out_specs=[vmem] * (parts + 1),
        scratch_shapes=[
            pltpu.SMEM((2, tile_total), jnp.int32),
            pltpu.VMEM((vec_count, set_count, row_total), jnp.bfloat16),
            *scratch,
            pltpu.SemaphoreType.DMA((2,)),
            pltpu.SemaphoreType.DMA((len(steps),)),
        ],
        compiler_params=pltpu.CompilerParams(vmem_limit_bytes=WIDE_BYTES),
        name="transposed_products",
    )(tile_count, *(pltpu.with_memory_space_constraint(x, pltpu.HBM) for x in (tile_pattern, vectors, tile_values)))
    back = [moved(m, lambda t: -offset(t), d) for d, m in enumerate(own)]
    keep, *across = pl.pallas_call(
        functools.partial(second_kernel, halves),
        out_shape=[message] * parts,
        in_specs=[smem] * 2 + [vmem] * (3 + parts),
        out_specs=[vmem] * parts,
        scratch_shapes=scratch,
        compiler_params=params,
        name="plain_products",
    )(tile_count, pattern, vectors, passed, tiles, *own)
    across = [moved(m, lambda t: 0, d + 1) for d, m in enumerate(across)]
    images = pl.pallas_call(
        functools.partial(last_kernel, parts),
        out_shape=jax.ShapeDtypeStruct((vec_count, set_count, row_total // parts), F32),
        in_specs=[vmem] * (2 * parts),
        out_specs=vmem,
        scratch_shapes=[pltpu.VMEM((held, columns, tile), F32)],
        compiler_params=params,
        name="sum_of_parts",
    )(keep, *across, *back)
    return images.transpose(1, 0, 2)


def solution(mesh):
    return jax.shard_map(
        local,
        mesh=mesh,
        in_specs=(
            P(None, None, "diag"),
            P("diag", "tri", None, None, None),
            P("diag", "tri", None, None),
            P("diag", "tri"),
        ),
        out_specs=P(None, None, ("diag", "tri")),
        check_vma=False,
    )
```

```python
import functools
import math

import jax
import jax.numpy as jnp
from jax import lax
from jax.experimental import pallas as pl
from jax.experimental.pallas import tpu as pltpu
from jax.sharding import PartitionSpec as P

F32 = jnp.float32
VMEM_BYTES = 16 << 20
WIDE_BYTES = 24 << 20
ROWS = 8
ORDER = 13
AHEAD = 3


def fill_vectors(vectors_ref, packed_ref, tile):
    blocks, padded, _ = packed_ref.shape
    vecs, sets, _ = vectors_ref.shape
    for b in range(blocks):
        slab = vectors_ref[:, :, b * tile : (b + 1) * tile].reshape(vecs * sets, tile)
        packed_ref[b] = jnp.concatenate(
            [slab, jnp.zeros((padded - vecs * sets, tile), slab.dtype)], axis=0
        )


def add_products(start, size, count, pattern_ref, source, target, packed_ref, tiles_ref, sums_ref):
    blocks, columns, tile = sums_ref.shape
    padded = packed_ref.shape[1]
    results = []
    for s in range(start, start + size, 2):
        left = jnp.concatenate([packed_ref[pattern_ref[source, s + e]] for e in range(2)], axis=0)
        right = jnp.concatenate([tiles_ref[s + e] for e in range(2)], axis=1)
        both = jnp.dot(left, right, preferred_element_type=F32)
        for e in range(2):
            place = jnp.where(s + e < count, pattern_ref[target, s + e], blocks - 1)
            results.append((place, both[e * padded : e * padded + columns, e * tile : (e + 1) * tile]))
    for place, part in results:
        sums_ref[place] += part


def write_message(message_ref, part):
    tile = part.shape[-1]
    flat = part.reshape(-1, ROWS, tile)
    top = jnp.max(jnp.abs(flat), axis=0)
    power = ORDER - jnp.floor(jnp.log2(jnp.maximum(top, 2.0**-100)))
    groups = flat.shape[0]
    message_ref[:groups] = flat * jnp.exp2(power)[None]
    message_ref[groups] = power


def read_message(message_ref, shape):
    groups = message_ref.shape[0] - 1
    return (message_ref[:groups] * jnp.exp2(-message_ref[groups])[None]).reshape(shape)


def first_kernel(steps, count_ref, pattern_hbm, vectors_hbm, tiles_hbm, *rest):
    turned_ref, *messages = rest[:-7]
    pattern_ref, vectors_ref, packed_ref, sums_ref, tiles_ref, small_sem, tile_sem = rest[-7:]
    parts = len(messages)
    blocks = packed_ref.shape[0]
    held = blocks // parts
    tri_index = lax.axis_index("tri")
    loads = [
        pltpu.make_async_copy(vectors_hbm, vectors_ref, small_sem.at[0]),
        pltpu.make_async_copy(pattern_hbm.at[0, 0], pattern_ref, small_sem.at[1]),
    ]
    streams = [
        pltpu.make_async_copy(
            tiles_hbm.at[0, 0, pl.ds(start, size)], tiles_ref.at[pl.ds(start, size)], tile_sem.at[k]
        )
        for k, (start, size) in enumerate(steps)
    ]
    for copy in loads + streams[:AHEAD]:
        copy.start()
    sums_ref[...] = jnp.zeros_like(sums_ref)
    for copy in loads:
        copy.wait()
    fill_vectors(vectors_ref, packed_ref, tiles_ref.shape[1])
    count = count_ref[0, 0]
    for k, (start, size) in enumerate(steps):
        streams[k].wait()
        if k + AHEAD < len(steps):
            streams[k + AHEAD].start()

        @pl.when(count > start)
        def _():
            add_products(
                start, size, count, pattern_ref, 0, 1, packed_ref, tiles_ref, sums_ref
            )
            for s in range(start, start + size):
                turned_ref[s] = tiles_ref[s].T

    for d, message_ref in enumerate(messages, 1):
        part = lax.rem(tri_index + d, parts)
        write_message(message_ref, sums_ref[pl.ds(part * held, held)])


def second_kernel(steps, count_ref, pattern_ref, vectors_ref, passed_ref, turned_ref, *rest):
    half = (len(rest) - 2) // 2
    own, (keep_ref, *messages), (packed_ref, sums_ref) = rest[:half], rest[half:-2], rest[-2:]
    parts = half
    blocks = packed_ref.shape[0]
    held = blocks // parts
    tri_index = lax.axis_index("tri")

    @pl.when(tri_index == 0)
    def _():
        for d, own_ref in enumerate(own, 1):
            d %= parts
            sums_ref[d * held : (d + 1) * held] = read_message(own_ref, keep_ref.shape)
        fill_vectors(vectors_ref, packed_ref, turned_ref.shape[1])

    @pl.when(tri_index != 0)
    def _():
        sums_ref[...] = jnp.zeros_like(sums_ref)
        fill_vectors(passed_ref, packed_ref, turned_ref.shape[1])

    count = count_ref[0, 0]
    for start, size in steps:

        @pl.when(count > start)
        def _():
            add_products(
                start, size, count, pattern_ref, 1, 0, packed_ref, turned_ref, sums_ref
            )

    keep_ref[...] = sums_ref[pl.ds(tri_index * held, held)]
    for d, message_ref in enumerate(messages, 1):
        part = lax.rem(tri_index + d, parts)
        write_message(message_ref, sums_ref[pl.ds(part * held, held)])


def last_kernel(parts, keep_ref, *rest):
    *messages, out_ref, total_ref = rest
    tri_index = lax.axis_index("tri")
    blocks, _, tile = keep_ref.shape
    total_ref[...] = keep_ref[...]
    for message_ref in messages[: parts - 1]:
        total_ref[...] += read_message(message_ref, keep_ref.shape)
    for d, message_ref in enumerate(messages[parts - 1 :], 1):

        @pl.when(lax.rem(tri_index + parts - d, parts) != 0)
        def _(message_ref=message_ref):
            total_ref[...] += read_message(message_ref, keep_ref.shape)

    vecs, sets, _ = out_ref.shape
    for b in range(blocks):
        out_ref[:, :, b * tile : (b + 1) * tile] = total_ref[b].reshape(vecs, sets, tile)


def local(trial_sets, tile_values, tile_pattern, tile_count):
    set_count, vec_count, row_total = trial_sets.shape
    columns = set_count * vec_count
    tile_total, tile = tile_values.shape[2:4]
    blocks = row_total // tile
    unit = math.gcd(tile_total, 48)
    steps = [(k * unit, unit) for k in range(tile_total // unit)]
    half = tile_total // 2
    halves = [(0, half), (half, half)]
    parts = lax.axis_size("tri")
    ring = lax.axis_size("diag")
    held = blocks // parts
    padded = -(-columns // 16) * 16
    message = pltpu.VMEM((held * columns // ROWS + 1, ROWS, tile), F32)
    smem, vmem, hbm = (pl.BlockSpec(memory_space=m) for m in (pltpu.SMEM, pltpu.VMEM, pltpu.HBM))
    scratch = [
        pltpu.VMEM((blocks, padded, tile), jnp.bfloat16),
        pltpu.VMEM((blocks + 1, columns, tile), F32),
    ]
    params = pltpu.CompilerParams(vmem_limit_bytes=VMEM_BYTES)

    def moved(x, way, turn):
        beside = lambda i: i ^ 1 if ring % 2 == 0 else i + 1
        pairs = [
            (
                i * parts + t,
                (beside(i) if t == turn == 0 else i + way * t) % ring * parts + (t + turn) % parts,
            )
            for i in range(ring)
            for t in range(parts)
        ]
        return lax.ppermute(x, ("diag", "tri"), pairs)

    def sent(x, way, turn):
        return moved(x.astype(jnp.float16), way, turn).astype(F32)

    vectors = trial_sets.transpose(1, 0, 2)
    passed = moved(vectors, 1, 0)
    pattern = tile_pattern.reshape(2, tile_total)
    turned, *own = pl.pallas_call(
        functools.partial(first_kernel, steps),
        out_shape=[pltpu.VMEM((tile_total, tile, tile), tile_values.dtype)] + [message] * parts,
        in_specs=[smem] + [hbm] * 3,
        out_specs=[vmem] * (parts + 1),
        scratch_shapes=[
            pltpu.SMEM((2, tile_total), jnp.int32),
            pltpu.VMEM((vec_count, set_count, row_total), jnp.bfloat16),
            *scratch,
            pltpu.VMEM((tile_total, tile, tile), tile_values.dtype),
            pltpu.SemaphoreType.DMA((2,)),
            pltpu.SemaphoreType.DMA((len(steps),)),
        ],
        compiler_params=pltpu.CompilerParams(vmem_limit_bytes=WIDE_BYTES),
        name="transposed_products",
    )(tile_count, *(pltpu.with_memory_space_constraint(x, pltpu.HBM) for x in (tile_pattern, vectors, tile_values)))
    back = [sent(m, -1, d % parts) for d, m in enumerate(own, 1)]
    keep, *across = pl.pallas_call(
        functools.partial(second_kernel, halves),
        out_shape=[pltpu.VMEM((held, columns, tile), F32)] + [message] * (parts - 1),
        in_specs=[smem] * 2 + [vmem] * (3 + parts),
        out_specs=[vmem] * parts,
        scratch_shapes=scratch,
        compiler_params=params,
        name="plain_products",
    )(tile_count, pattern, vectors, passed, turned, *own)
    across = [sent(m, 0, d + 1) for d, m in enumerate(across)]
    images = pl.pallas_call(
        functools.partial(last_kernel, parts),
        out_shape=jax.ShapeDtypeStruct((vec_count, set_count, row_total // parts), F32),
        in_specs=[vmem] * (2 * parts),
        out_specs=vmem,
        scratch_shapes=[pltpu.VMEM((held, columns, tile), F32)],
        compiler_params=params,
        name="sum_of_parts",
    )(keep, *across, *back)
    return images.transpose(1, 0, 2)


def solution(mesh):
    return jax.shard_map(
        local,
        mesh=mesh,
        in_specs=(
            P(None, None, "diag"),
            P("diag", "tri", None, None, None),
            P("diag", "tri", None, None),
            P("diag", "tri"),
        ),
        out_specs=P(None, None, ("diag", "tri")),
        check_vma=False,
    )
```

```python
import functools
import math

import jax
import jax.numpy as jnp
from jax import lax
from jax.experimental import pallas as pl
from jax.experimental.pallas import tpu as pltpu
from jax.sharding import PartitionSpec as P

F32 = jnp.float32
VMEM_BYTES = 16 << 20
WIDE_BYTES = 24 << 20
ROWS = 8
ORDER = 13
AHEAD = 3


def fill_vectors(vectors_ref, packed_ref, tile):
    blocks, padded, _ = packed_ref.shape
    vecs, sets, _ = vectors_ref.shape
    for b in range(blocks):
        slab = vectors_ref[:, :, b * tile : (b + 1) * tile].reshape(vecs * sets, tile)
        packed_ref[b] = jnp.concatenate(
            [slab, jnp.zeros((padded - vecs * sets, tile), slab.dtype)], axis=0
        )


def add_products(start, size, count, pattern_ref, source, target, packed_ref, tiles_ref, sums_ref):
    blocks, columns, tile = sums_ref.shape
    padded = packed_ref.shape[1]
    results = []
    for s in range(start, start + size, 2):
        left = jnp.concatenate([packed_ref[pattern_ref[source, s + e]] for e in range(2)], axis=0)
        right = jnp.concatenate([tiles_ref[s + e] for e in range(2)], axis=1)
        both = jnp.dot(left, right, preferred_element_type=F32)
        places = [jnp.where(s + e < count, pattern_ref[target, s + e], blocks - 1) for e in range(2)]
        parts = [both[e * padded : e * padded + columns, e * tile : (e + 1) * tile] for e in range(2)]
        results.append((places, parts))
    for (place, other), (part, last) in results:
        held, total = sums_ref[place], sums_ref[other]
        sums_ref[place] = held + part
        sums_ref[other] = total + (last + jnp.where(place == other, part, 0.0))


def write_message(message_ref, part):
    tile = part.shape[-1]
    flat = part.reshape(-1, ROWS, tile)
    top = jnp.max(jnp.abs(flat), axis=0)
    power = ORDER - jnp.floor(jnp.log2(jnp.maximum(top, 2.0**-100)))
    groups = flat.shape[0]
    message_ref[:groups] = flat * jnp.exp2(power)[None]
    message_ref[groups] = power


def read_message(message_ref, shape):
    groups = message_ref.shape[0] - 1
    return (message_ref[:groups] * jnp.exp2(-message_ref[groups])[None]).reshape(shape)


def first_kernel(steps, count_ref, pattern_hbm, vectors_hbm, tiles_hbm, *rest):
    turned_ref, *messages = rest[:-7]
    pattern_ref, vectors_ref, packed_ref, sums_ref, tiles_ref, small_sem, tile_sem = rest[-7:]
    parts = len(messages)
    blocks = packed_ref.shape[0]
    held = blocks // parts
    tri_index = lax.axis_index("tri")
    loads = [
        pltpu.make_async_copy(vectors_hbm, vectors_ref, small_sem.at[0]),
        pltpu.make_async_copy(pattern_hbm.at[0, 0], pattern_ref, small_sem.at[1]),
    ]
    streams = [
        pltpu.make_async_copy(
            tiles_hbm.at[0, 0, pl.ds(start, size)], tiles_ref.at[pl.ds(start, size)], tile_sem.at[k]
        )
        for k, (start, size) in enumerate(steps)
    ]
    for copy in loads + streams[:AHEAD]:
        copy.start()
    sums_ref[...] = jnp.zeros_like(sums_ref)
    for copy in loads:
        copy.wait()
    fill_vectors(vectors_ref, packed_ref, tiles_ref.shape[1])
    count = count_ref[0, 0]
    for k, (start, size) in enumerate(steps):
        streams[k].wait()
        if k + AHEAD < len(steps):
            streams[k + AHEAD].start()

        @pl.when(count > start)
        def _():
            add_products(
                start, size, count, pattern_ref, 0, 1, packed_ref, tiles_ref, sums_ref
            )
            for s in range(start, start + size):
                turned_ref[s] = tiles_ref[s].T

    for d, message_ref in enumerate(messages, 1):
        part = lax.rem(tri_index + d, parts)
        write_message(message_ref, sums_ref[pl.ds(part * held, held)])


def second_kernel(steps, count_ref, pattern_ref, vectors_ref, passed_ref, turned_ref, *rest):
    parts = (len(rest) - 2) // 3
    own, (keep_ref, *messages), (packed_ref, sums_ref) = rest[:parts], rest[parts:-2], rest[-2:]
    messages, later = messages[: parts - 1], messages[parts - 1 :]
    blocks = packed_ref.shape[0]
    held = blocks // parts
    tri_index = lax.axis_index("tri")

    @pl.when(tri_index == 0)
    def _():
        for d, own_ref in enumerate(own, 1):
            d %= parts
            sums_ref[d * held : (d + 1) * held] = read_message(own_ref, keep_ref.shape)
        fill_vectors(vectors_ref, packed_ref, turned_ref.shape[1])

    @pl.when(tri_index != 0)
    def _():
        sums_ref[...] = jnp.zeros_like(sums_ref)
        fill_vectors(passed_ref, packed_ref, turned_ref.shape[1])

    count = count_ref[0, 0]
    for start, size in steps:

        @pl.when(count > start)
        def _():
            add_products(
                start, size, count, pattern_ref, 1, 0, packed_ref, turned_ref, sums_ref
            )

    keep_ref[...] = sums_ref[pl.ds(tri_index * held, held)]
    for d, message_ref in enumerate(messages, 1):
        part = lax.rem(tri_index + d, parts)
        write_message(message_ref, sums_ref[pl.ds(part * held, held)])
    for own_ref, later_ref in zip(own, later):
        later_ref[...] = own_ref[...]

    @pl.when(tri_index == 0)
    def _():
        for message_ref, later_ref in zip(messages, later):
            later_ref[...] = message_ref[...]


def add_kernel(skipped, kept_ref, *rest):
    *messages, total_ref = rest
    tri_index = lax.axis_index("tri")
    total_ref[...] = kept_ref[...]
    for skip, message_ref in zip(skipped, messages):

        @pl.when(tri_index != skip)
        def _(message_ref=message_ref):
            total_ref[...] += read_message(message_ref, kept_ref.shape)


def last_kernel(kept_ref, message_ref, out_ref, total_ref):
    blocks, _, tile = kept_ref.shape
    total_ref[...] = kept_ref[...]

    @pl.when(lax.axis_index("tri") != 0)
    def _():
        total_ref[...] += read_message(message_ref, kept_ref.shape)

    vecs, sets, _ = out_ref.shape
    for b in range(blocks):
        out_ref[:, :, b * tile : (b + 1) * tile] = total_ref[b].reshape(vecs, sets, tile)


def local(trial_sets, tile_values, tile_pattern, tile_count):
    set_count, vec_count, row_total = trial_sets.shape
    columns = set_count * vec_count
    tile_total, tile = tile_values.shape[2:4]
    blocks = row_total // tile
    unit = math.gcd(tile_total, 48)
    steps = [(k * unit, unit) for k in range(tile_total // unit)]
    half = tile_total // 2
    halves = [(0, half), (half, half)]
    parts = lax.axis_size("tri")
    ring = lax.axis_size("diag")
    held = blocks // parts
    padded = -(-columns // 16) * 16
    message = pltpu.VMEM((held * columns // ROWS + 1, ROWS, tile), F32)
    smem, vmem, hbm = (pl.BlockSpec(memory_space=m) for m in (pltpu.SMEM, pltpu.VMEM, pltpu.HBM))
    scratch = [
        pltpu.VMEM((blocks, padded, tile), jnp.bfloat16),
        pltpu.VMEM((blocks + 1, columns, tile), F32),
    ]
    params = pltpu.CompilerParams(vmem_limit_bytes=VMEM_BYTES)

    def moved(x, way, turn, swap=lambda i: i):
        pairs = [
            (i * parts + t, ((i + way * t) % ring if t else swap(i)) * parts + (t + turn) % parts)
            for i in range(ring)
            for t in range(parts)
        ]
        return lax.ppermute(x, ("diag", "tri"), pairs)

    def beside(i):
        return i ^ 1 if ring % 2 == 0 else (i + 1) % ring

    def aside(i):
        step = ring // 4
        return {0: 1, 1: step + 1, step + 1: step, step: 0}.get(i, i) if step > 1 else i

    def sent(x, *route):
        return moved(x.astype(jnp.float16), *route).astype(F32)

    vectors = trial_sets.transpose(1, 0, 2)
    passed = moved(vectors, 1, 0, beside)
    pattern = tile_pattern.reshape(2, tile_total)
    turned, *own = pl.pallas_call(
        functools.partial(first_kernel, steps),
        out_shape=[pltpu.VMEM((tile_total, tile, tile), tile_values.dtype)] + [message] * parts,
        in_specs=[smem] + [hbm] * 3,
        out_specs=[vmem] * (parts + 1),
        scratch_shapes=[
            pltpu.SMEM((2, tile_total), jnp.int32),
            pltpu.VMEM((vec_count, set_count, row_total), jnp.bfloat16),
            *scratch,
            pltpu.VMEM((tile_total, tile, tile), tile_values.dtype),
            pltpu.SemaphoreType.DMA((2,)),
            pltpu.SemaphoreType.DMA((len(steps),)),
        ],
        compiler_params=pltpu.CompilerParams(vmem_limit_bytes=WIDE_BYTES),
        name="transposed_products",
    )(tile_count, *(pltpu.with_memory_space_constraint(x, pltpu.HBM) for x in (tile_pattern, vectors, tile_values)))
    keep, *rest = pl.pallas_call(
        functools.partial(second_kernel, halves),
        out_shape=[pltpu.VMEM((held, columns, tile), F32)] + [message] * (2 * parts - 1),
        in_specs=[smem] * 2 + [vmem] * (3 + parts),
        out_specs=[vmem] * (2 * parts),
        scratch_shapes=scratch,
        compiler_params=params,
        name="plain_products",
    )(tile_count, pattern, vectors, passed, turned, *own)
    across = [sent(m, 0, d, aside) for d, m in enumerate(rest[: parts - 1], 1)]
    back = [sent(m, -1, d) for d, m in enumerate(rest[parts - 1 : -1], 1)]
    back.append(sent(rest[-1], -1, 0, beside))

    def added(skipped, kept, messages):
        return pl.pallas_call(
            functools.partial(add_kernel, skipped),
            out_shape=pltpu.VMEM((held, columns, tile), F32),
            in_specs=[vmem] * (len(messages) + 1),
            out_specs=vmem,
            compiler_params=params,
            name="sum_of_messages",
        )(kept, *messages)

    kept = added([d % parts for d in range(1, parts)], keep, across)
    kept = added([-1] * (parts - 1), kept, back[:-1])
    images = pl.pallas_call(
        last_kernel,
        out_shape=jax.ShapeDtypeStruct((vec_count, set_count, row_total // parts), F32),
        in_specs=[vmem] * 2,
        out_specs=vmem,
        scratch_shapes=[pltpu.VMEM((held, columns, tile), F32)],
        compiler_params=params,
        name="last_sum",
    )(kept, back[-1])
    return images.transpose(1, 0, 2)


def solution(mesh):
    return jax.shard_map(
        local,
        mesh=mesh,
        in_specs=(
            P(None, None, "diag"),
            P("diag", "tri", None, None, None),
            P("diag", "tri", None, None),
            P("diag", "tri"),
        ),
        out_specs=P(None, None, ("diag", "tri")),
        check_vma=False,
    )
```

```python
import functools
import math

import jax
import jax.numpy as jnp
from jax import lax
from jax.experimental import pallas as pl
from jax.experimental.pallas import tpu as pltpu
from jax.sharding import PartitionSpec as P

F32 = jnp.float32
VMEM_BYTES = 16 << 20
WIDE_BYTES = 24 << 20
ROWS = 8
ORDER = 13
AHEAD = 3


def fill_vectors(vectors_ref, packed_ref, tile):
    blocks, padded, _ = packed_ref.shape
    vecs, sets, _ = vectors_ref.shape
    for b in range(blocks):
        slab = vectors_ref[:, :, b * tile : (b + 1) * tile].reshape(vecs * sets, tile)
        packed_ref[b] = jnp.concatenate(
            [slab, jnp.zeros((padded - vecs * sets, tile), slab.dtype)], axis=0
        )


def add_products(start, size, count, pattern_ref, source, target, packed_ref, tiles_ref, sums_ref):
    blocks, columns, tile = sums_ref.shape
    padded = packed_ref.shape[1]
    results = []
    for s in range(start, start + size, 2):
        left = jnp.concatenate([packed_ref[pattern_ref[source, s + e]] for e in range(2)], axis=0)
        right = jnp.concatenate([tiles_ref[s + e] for e in range(2)], axis=1)
        both = jnp.dot(left, right, preferred_element_type=F32)
        places = [jnp.where(s + e < count, pattern_ref[target, s + e], blocks - 1) for e in range(2)]
        parts = [both[e * padded : e * padded + columns, e * tile : (e + 1) * tile] for e in range(2)]
        results.append((places, parts))
    for (place, other), (part, last) in results:
        held, total = sums_ref[place], sums_ref[other]
        sums_ref[place] = held + part
        sums_ref[other] = total + (last + jnp.where(place == other, part, 0.0))


def write_message(message_ref, part):
    tile = part.shape[-1]
    flat = part.reshape(-1, ROWS, tile)
    top = jnp.max(jnp.abs(flat), axis=0)
    power = ORDER - jnp.floor(jnp.log2(jnp.maximum(top, 2.0**-100)))
    groups = flat.shape[0]
    message_ref[:groups] = flat * jnp.exp2(power)[None]
    message_ref[groups] = power


def read_message(message_ref, shape):
    groups = message_ref.shape[0] - 1
    return (message_ref[:groups] * jnp.exp2(-message_ref[groups])[None]).reshape(shape)


def first_kernel(steps, count_ref, pattern_hbm, vectors_hbm, tiles_hbm, *rest):
    turned_ref, *messages = rest[:-7]
    pattern_ref, vectors_ref, packed_ref, sums_ref, tiles_ref, small_sem, tile_sem = rest[-7:]
    parts = len(messages)
    blocks = packed_ref.shape[0]
    held = blocks // parts
    tri_index = lax.axis_index("tri")
    loads = [
        pltpu.make_async_copy(vectors_hbm, vectors_ref, small_sem.at[0]),
        pltpu.make_async_copy(pattern_hbm.at[0, 0], pattern_ref, small_sem.at[1]),
    ]
    streams = [
        pltpu.make_async_copy(
            tiles_hbm.at[0, 0, pl.ds(start, size)], tiles_ref.at[pl.ds(start, size)], tile_sem.at[k]
        )
        for k, (start, size) in enumerate(steps)
    ]
    for copy in loads + streams[:AHEAD]:
        copy.start()
    sums_ref[...] = jnp.zeros_like(sums_ref)
    for copy in loads:
        copy.wait()
    fill_vectors(vectors_ref, packed_ref, tiles_ref.shape[1])
    count = count_ref[0, 0]
    for k, (start, size) in enumerate(steps):
        streams[k].wait()
        if k + AHEAD < len(steps):
            streams[k + AHEAD].start()

        @pl.when(count > start)
        def _():
            add_products(
                start, size, count, pattern_ref, 0, 1, packed_ref, tiles_ref, sums_ref
            )
            for s in range(start, start + size):
                turned_ref[s] = tiles_ref[s].T

    for d, message_ref in enumerate(messages, 1):
        part = lax.rem(tri_index + d, parts)
        write_message(message_ref, sums_ref[pl.ds(part * held, held)])


def second_kernel(steps, count_ref, pattern_ref, vectors_ref, passed_ref, turned_ref, *rest):
    parts = (len(rest) - 2) // 3
    own, (keep_ref, *messages), (packed_ref, sums_ref) = rest[:parts], rest[parts:-2], rest[-2:]
    messages, later = messages[: parts - 1], messages[parts - 1 :]
    blocks = packed_ref.shape[0]
    held = blocks // parts
    tri_index = lax.axis_index("tri")

    @pl.when(tri_index == 0)
    def _():
        for d, own_ref in enumerate(own, 1):
            d %= parts
            sums_ref[d * held : (d + 1) * held] = read_message(own_ref, keep_ref.shape)
        fill_vectors(vectors_ref, packed_ref, turned_ref.shape[1])

    @pl.when(tri_index != 0)
    def _():
        sums_ref[...] = jnp.zeros_like(sums_ref)
        fill_vectors(passed_ref, packed_ref, turned_ref.shape[1])

    count = count_ref[0, 0]
    for fewest, size in steps:

        @pl.when((count > fewest) & (count <= size))
        def _():
            add_products(
                0, size, count, pattern_ref, 1, 0, packed_ref, turned_ref, sums_ref
            )

    keep_ref[...] = sums_ref[pl.ds(tri_index * held, held)]
    for d, message_ref in enumerate(messages, 1):
        part = lax.rem(tri_index + d, parts)
        write_message(message_ref, sums_ref[pl.ds(part * held, held)])

    @pl.when(tri_index == 0)
    def _():
        for message_ref, later_ref in zip(messages, later):
            later_ref[...] = message_ref[...]


def add_kernel(skipped, kept_ref, *rest):
    *messages, total_ref = rest
    tri_index = lax.axis_index("tri")
    total_ref[...] = kept_ref[...]
    for skip, message_ref in zip(skipped, messages):

        @pl.when(tri_index != skip)
        def _(message_ref=message_ref):
            total_ref[...] += read_message(message_ref, kept_ref.shape)


def last_kernel(kept_ref, message_ref, out_ref, total_ref):
    blocks, _, tile = kept_ref.shape
    total_ref[...] = kept_ref[...]

    @pl.when(lax.axis_index("tri") != 0)
    def _():
        total_ref[...] += read_message(message_ref, kept_ref.shape)

    vecs, sets, _ = out_ref.shape
    for b in range(blocks):
        out_ref[:, :, b * tile : (b + 1) * tile] = total_ref[b].reshape(vecs, sets, tile)


def local(trial_sets, tile_values, tile_pattern, tile_count):
    set_count, vec_count, row_total = trial_sets.shape
    columns = set_count * vec_count
    tile_total, tile = tile_values.shape[2:4]
    blocks = row_total // tile
    unit = math.gcd(tile_total, 48)
    steps = [(k * unit, unit) for k in range(tile_total // unit)]
    half = tile_total // 2
    halves = [(0, half), (half, tile_total)]
    parts = lax.axis_size("tri")
    ring = lax.axis_size("diag")
    held = blocks // parts
    padded = -(-columns // 16) * 16
    message = pltpu.VMEM((held * columns // ROWS + 1, ROWS, tile), F32)
    smem, vmem, hbm = (pl.BlockSpec(memory_space=m) for m in (pltpu.SMEM, pltpu.VMEM, pltpu.HBM))
    scratch = [
        pltpu.VMEM((blocks, padded, tile), jnp.bfloat16),
        pltpu.VMEM((blocks + 1, columns, tile), F32),
    ]
    params = pltpu.CompilerParams(vmem_limit_bytes=VMEM_BYTES)

    def moved(x, way, turn, swap=lambda i: i):
        pairs = [
            (i * parts + t, ((i + way * t) % ring if t else swap(i)) * parts + (t + turn) % parts)
            for i in range(ring)
            for t in range(parts)
        ]
        return lax.ppermute(x, ("diag", "tri"), pairs)

    def beside(i):
        return i ^ 1 if ring % 2 == 0 else (i + 1) % ring

    def aside(i):
        step = ring // 4
        return {0: 1, 1: step + 1, step + 1: step, step: 0}.get(i, i) if step > 1 else i

    def sent(x, *route):
        return moved(x.astype(jnp.float16), *route).astype(F32)

    vectors = trial_sets.transpose(1, 0, 2)
    passed = moved(vectors, 1, 0, beside)
    pattern = tile_pattern.reshape(2, tile_total)
    turned, *own = pl.pallas_call(
        functools.partial(first_kernel, steps),
        out_shape=[pltpu.VMEM((tile_total, tile, tile), tile_values.dtype)] + [message] * parts,
        in_specs=[smem] + [hbm] * 3,
        out_specs=[vmem] * (parts + 1),
        scratch_shapes=[
            pltpu.SMEM((2, tile_total), jnp.int32),
            pltpu.VMEM((vec_count, set_count, row_total), jnp.bfloat16),
            *scratch,
            pltpu.VMEM((tile_total, tile, tile), tile_values.dtype),
            pltpu.SemaphoreType.DMA((2,)),
            pltpu.SemaphoreType.DMA((len(steps),)),
        ],
        compiler_params=pltpu.CompilerParams(vmem_limit_bytes=WIDE_BYTES),
        name="transposed_products",
    )(tile_count, *(pltpu.with_memory_space_constraint(x, pltpu.HBM) for x in (tile_pattern, vectors, tile_values)))
    keep, *rest = pl.pallas_call(
        functools.partial(second_kernel, halves),
        out_shape=[pltpu.VMEM((held, columns, tile), F32)] + [message] * (2 * parts - 1),
        in_specs=[smem] * 2 + [vmem] * (3 + parts),
        out_specs=[vmem] * (2 * parts),
        scratch_shapes=scratch,
        input_output_aliases={5 + d: parts + d for d in range(parts)},
        compiler_params=params,
        name="plain_products",
    )(tile_count, pattern, vectors, passed, turned, *own)
    across = [sent(m, 0, d, aside) for d, m in enumerate(rest[: parts - 1], 1)]
    back = [sent(m, -1, d) for d, m in enumerate(rest[parts - 1 : -1], 1)]
    back.append(sent(rest[-1], -1, 0, beside))

    def added(skipped, kept, messages):
        return pl.pallas_call(
            functools.partial(add_kernel, skipped),
            out_shape=pltpu.VMEM((held, columns, tile), F32),
            in_specs=[vmem] * (len(messages) + 1),
            out_specs=vmem,
            compiler_params=params,
            name="sum_of_messages",
        )(kept, *messages)

    kept = added([d % parts for d in range(1, parts)], keep, across)
    kept = added([-1] * (parts - 1), kept, back[:-1])
    images = pl.pallas_call(
        last_kernel,
        out_shape=jax.ShapeDtypeStruct((vec_count, set_count, row_total // parts), F32),
        in_specs=[vmem] * 2,
        out_specs=vmem,
        scratch_shapes=[pltpu.VMEM((held, columns, tile), F32)],
        compiler_params=params,
        name="last_sum",
    )(kept, back[-1])
    return images.transpose(1, 0, 2)


def solution(mesh):
    return jax.shard_map(
        local,
        mesh=mesh,
        in_specs=(
            P(None, None, "diag"),
            P("diag", "tri", None, None, None),
            P("diag", "tri", None, None),
            P("diag", "tri"),
        ),
        out_specs=P(None, None, ("diag", "tri")),
        check_vma=False,
    )
```

```python
import functools
import math

import jax
import jax.numpy as jnp
from jax import lax
from jax.experimental import pallas as pl
from jax.experimental.pallas import tpu as pltpu
from jax.sharding import PartitionSpec as P

F32 = jnp.float32
VMEM_BYTES = 16 << 20
WIDE_BYTES = 24 << 20
ROWS = 8
ORDER = 13
AHEAD = 3


def fill_vectors(vectors_ref, packed_ref, tile):
    blocks, padded, _ = packed_ref.shape
    vecs, sets, _ = vectors_ref.shape
    for b in range(blocks):
        slab = vectors_ref[:, :, b * tile : (b + 1) * tile].reshape(vecs * sets, tile)
        packed_ref[b] = jnp.concatenate(
            [slab, jnp.zeros((padded - vecs * sets, tile), slab.dtype)], axis=0
        )


def add_products(start, size, count, pattern_ref, source, target, packed_ref, tiles_ref, sums_ref):
    blocks, columns, tile = sums_ref.shape
    padded = packed_ref.shape[1]
    results = []
    for s in range(start, start + size, 2):
        left = jnp.concatenate([packed_ref[pattern_ref[source, s + e]] for e in range(2)], axis=0)
        right = jnp.concatenate([tiles_ref[s + e] for e in range(2)], axis=1)
        both = jnp.dot(left, right, preferred_element_type=F32)
        places = [jnp.where(s + e < count, pattern_ref[target, s + e], blocks - 1) for e in range(2)]
        parts = [both[e * padded : e * padded + columns, e * tile : (e + 1) * tile] for e in range(2)]
        results.append((places, parts))
    for (place, other), (part, last) in results:
        held, total = sums_ref[place], sums_ref[other]
        sums_ref[place] = held + part
        sums_ref[other] = total + (last + jnp.where(place == other, part, 0.0))


def write_message(message_ref, part):
    tile = part.shape[-1]
    flat = part.reshape(-1, ROWS, tile)
    top = jnp.max(jnp.abs(flat), axis=0)
    power = ORDER - jnp.floor(jnp.log2(jnp.maximum(top, 2.0**-100)))
    groups = flat.shape[0]
    message_ref[:groups] = flat * jnp.exp2(power)[None]
    message_ref[groups] = power


def read_message(message_ref, shape):
    groups = message_ref.shape[0] - 1
    return (message_ref[:groups] * jnp.exp2(-message_ref[groups])[None]).reshape(shape)


def first_kernel(steps, count_ref, pattern_hbm, vectors_hbm, tiles_hbm, *rest):
    turned_ref, *messages = rest[:-7]
    pattern_ref, vectors_ref, packed_ref, sums_ref, tiles_ref, small_sem, tile_sem = rest[-7:]
    parts = len(messages)
    blocks = packed_ref.shape[0]
    held = blocks // parts
    tri_index = lax.axis_index("tri")
    loads = [
        pltpu.make_async_copy(vectors_hbm, vectors_ref, small_sem.at[0]),
        pltpu.make_async_copy(pattern_hbm.at[0, 0], pattern_ref, small_sem.at[1]),
    ]
    streams = [
        pltpu.make_async_copy(
            tiles_hbm.at[0, 0, pl.ds(start, size)], tiles_ref.at[pl.ds(start, size)], tile_sem.at[k]
        )
        for k, (start, size) in enumerate(steps)
    ]
    count = count_ref[0, 0]

    def begin(k):
        @pl.when(count > steps[k][0])
        def _():
            streams[k].start()

    for copy in loads:
        copy.start()
    for k in range(min(AHEAD, len(steps))):
        begin(k)
    sums_ref[...] = jnp.zeros_like(sums_ref)
    for copy in loads:
        copy.wait()
    fill_vectors(vectors_ref, packed_ref, tiles_ref.shape[1])
    for k, (start, size) in enumerate(steps):

        @pl.when(count > start)
        def _():
            streams[k].wait()
            if k + AHEAD < len(steps):
                begin(k + AHEAD)
            add_products(
                start, size, count, pattern_ref, 0, 1, packed_ref, tiles_ref, sums_ref
            )
            for s in range(start, start + size):
                turned_ref[s] = tiles_ref[s].T

    for d, message_ref in enumerate(messages, 1):
        part = lax.rem(tri_index + d, parts)
        write_message(message_ref, sums_ref[pl.ds(part * held, held)])


def second_kernel(steps, count_ref, pattern_ref, vectors_ref, passed_ref, turned_ref, *rest):
    parts = (len(rest) - 2) // 3
    own, (keep_ref, *messages), (packed_ref, sums_ref) = rest[:parts], rest[parts:-2], rest[-2:]
    messages, later = messages[: parts - 1], messages[parts - 1 :]
    blocks = packed_ref.shape[0]
    held = blocks // parts
    tri_index = lax.axis_index("tri")

    @pl.when(tri_index == 0)
    def _():
        for d, own_ref in enumerate(own, 1):
            d %= parts
            sums_ref[d * held : (d + 1) * held] = read_message(own_ref, keep_ref.shape)
        fill_vectors(vectors_ref, packed_ref, turned_ref.shape[1])

    @pl.when(tri_index != 0)
    def _():
        sums_ref[...] = jnp.zeros_like(sums_ref)
        fill_vectors(passed_ref, packed_ref, turned_ref.shape[1])

    count = count_ref[0, 0]
    for fewest, size in steps:

        @pl.when((count > fewest) & (count <= size))
        def _():
            add_products(
                0, size, count, pattern_ref, 1, 0, packed_ref, turned_ref, sums_ref
            )

    keep_ref[...] = sums_ref[pl.ds(tri_index * held, held)]
    for d, message_ref in enumerate(messages, 1):
        part = lax.rem(tri_index + d, parts)
        write_message(message_ref, sums_ref[pl.ds(part * held, held)])

    @pl.when(tri_index == 0)
    def _():
        for message_ref, later_ref in zip(messages, later):
            later_ref[...] = message_ref[...]


def add_kernel(skipped, kept_ref, *rest):
    *messages, total_ref = rest
    tri_index = lax.axis_index("tri")
    total_ref[...] = kept_ref[...]
    for skip, message_ref in zip(skipped, messages):

        @pl.when(tri_index != skip)
        def _(message_ref=message_ref):
            total_ref[...] += read_message(message_ref, kept_ref.shape)


def last_kernel(kept_ref, message_ref, out_ref, total_ref):
    blocks, _, tile = kept_ref.shape
    total_ref[...] = kept_ref[...]

    @pl.when(lax.axis_index("tri") != 0)
    def _():
        total_ref[...] += read_message(message_ref, kept_ref.shape)

    vecs, sets, _ = out_ref.shape
    for b in range(blocks):
        out_ref[:, :, b * tile : (b + 1) * tile] = total_ref[b].reshape(vecs, sets, tile)


def local(trial_sets, tile_values, tile_pattern, tile_count):
    set_count, vec_count, row_total = trial_sets.shape
    columns = set_count * vec_count
    tile_total, tile = tile_values.shape[2:4]
    blocks = row_total // tile
    unit = math.gcd(tile_total, 48)
    steps = [(k * unit, unit) for k in range(tile_total // unit)]
    half = tile_total // 2
    halves = [(0, half), (half, tile_total)]
    parts = lax.axis_size("tri")
    ring = lax.axis_size("diag")
    held = blocks // parts
    padded = -(-columns // 16) * 16
    message = pltpu.VMEM((held * columns // ROWS + 1, ROWS, tile), F32)
    smem, vmem, hbm = (pl.BlockSpec(memory_space=m) for m in (pltpu.SMEM, pltpu.VMEM, pltpu.HBM))
    scratch = [
        pltpu.VMEM((blocks, padded, tile), jnp.bfloat16),
        pltpu.VMEM((blocks + 1, columns, tile), F32),
    ]
    params = pltpu.CompilerParams(vmem_limit_bytes=VMEM_BYTES)

    def moved(x, way, turn, swap=lambda i: i):
        pairs = [
            (i * parts + t, ((i + way * t) % ring if t else swap(i)) * parts + (t + turn) % parts)
            for i in range(ring)
            for t in range(parts)
        ]
        return lax.ppermute(x, ("diag", "tri"), pairs)

    def beside(i):
        return i ^ 1 if ring % 2 == 0 else (i + 1) % ring

    def aside(i):
        step = ring // 4
        return {0: 1, 1: step + 1, step + 1: step, step: 0}.get(i, i) if step > 1 else i

    def sent(x, *route):
        return moved(x.astype(jnp.float16), *route).astype(F32)

    vectors = trial_sets.transpose(1, 0, 2)
    passed = moved(vectors, 1, 0, beside)
    pattern = tile_pattern.reshape(2, tile_total)
    turned, *own = pl.pallas_call(
        functools.partial(first_kernel, steps),
        out_shape=[pltpu.VMEM((tile_total, tile, tile), tile_values.dtype)] + [message] * parts,
        in_specs=[smem] + [hbm] * 3,
        out_specs=[vmem] * (parts + 1),
        scratch_shapes=[
            pltpu.SMEM((2, tile_total), jnp.int32),
            pltpu.VMEM((vec_count, set_count, row_total), jnp.bfloat16),
            *scratch,
            pltpu.VMEM((tile_total, tile, tile), tile_values.dtype),
            pltpu.SemaphoreType.DMA((2,)),
            pltpu.SemaphoreType.DMA((len(steps),)),
        ],
        compiler_params=pltpu.CompilerParams(vmem_limit_bytes=WIDE_BYTES),
        name="transposed_products",
    )(tile_count, *(pltpu.with_memory_space_constraint(x, pltpu.HBM) for x in (tile_pattern, vectors, tile_values)))
    keep, *rest = pl.pallas_call(
        functools.partial(second_kernel, halves),
        out_shape=[pltpu.VMEM((held, columns, tile), F32)] + [message] * (2 * parts - 1),
        in_specs=[smem] * 2 + [vmem] * (3 + parts),
        out_specs=[vmem] * (2 * parts),
        scratch_shapes=scratch,
        input_output_aliases={5 + d: parts + d for d in range(parts)},
        compiler_params=params,
        name="plain_products",
    )(tile_count, pattern, vectors, passed, turned, *own)
    across = [sent(m, 0, d, aside) for d, m in enumerate(rest[: parts - 1], 1)]
    back = [sent(m, -1, d) for d, m in enumerate(rest[parts - 1 : -1], 1)]
    back.append(sent(rest[-1], -1, 0, beside))

    def added(skipped, kept, messages):
        return pl.pallas_call(
            functools.partial(add_kernel, skipped),
            out_shape=pltpu.VMEM((held, columns, tile), F32),
            in_specs=[vmem] * (len(messages) + 1),
            out_specs=vmem,
            compiler_params=params,
            name="sum_of_messages",
        )(kept, *messages)

    kept = added([d % parts for d in range(1, parts)], keep, across)
    kept = added([-1] * (parts - 1), kept, back[:-1])
    images = pl.pallas_call(
        last_kernel,
        out_shape=jax.ShapeDtypeStruct((vec_count, set_count, row_total // parts), F32),
        in_specs=[vmem] * 2,
        out_specs=vmem,
        scratch_shapes=[pltpu.VMEM((held, columns, tile), F32)],
        compiler_params=params,
        name="last_sum",
    )(kept, back[-1])
    return images.transpose(1, 0, 2)


def solution(mesh):
    return jax.shard_map(
        local,
        mesh=mesh,
        in_specs=(
            P(None, None, "diag"),
            P("diag", "tri", None, None, None),
            P("diag", "tri", None, None),
            P("diag", "tri"),
        ),
        out_specs=P(None, None, ("diag", "tri")),
        check_vma=False,
    )
```
